128 devices in a mesh: lat: 16 (over x, y_hi, core), lon: 8 (over y_lo, z).
Axes of the slice: x: 4, y: 4 (y_hi: 2, y_lo: 2; y = y_hi * 2 + y_lo), z: 4, core: 2. Of those that a mesh axis runs over, the one named last changes fastest.
Arguments:
- tokens: bfloat16 [256, 2048, 256], P('lat', 'lon'), may hold values from -16 to 16
- w_qkv: bfloat16 [256, 768], replicated, may hold values from -0.375 to 0.375
- w_out: bfloat16 [256, 256], replicated, may hold values from -0.375 to 0.375
Outputs:
- attended: bfloat16 [256, 2048, 256], P('lat', 'lon')
The draws below stay inside these ranges and needn't reach their ends.
All inputs are finite; a program needn't handle non-finite values.
Results may differ from the reference program's by a relative error of at most 0.011.
Values may be sent and summed in bfloat16 or wider, within the bound.
No kernel may reach another device: no remote copies, remote signals or barrier semaphores. Data moves between devices by JAX's collectives and lax.ppermute only.
A program may use at most 320 MiB of HBM per device.

```python
import math
import jax
import jax.numpy as jnp
from jax import lax

D = 256
HEADS = 8
GRID = 8
H = 256
W = 2048


def draw_tokens(key, part):
    key = jax.random.fold_in(key, 11)
    key_base = jax.random.fold_in(key, 0)
    base = jax.random.normal(key_base, (H, W, D), jnp.float32)
    values = jnp.clip(base, -6.0, 6.0)
    return values.astype(jnp.bfloat16)


def scatter_about(rng, extent, deviation, reach, kind=jnp.bfloat16):
    entries = deviation * jax.random.normal(rng, extent, jnp.float32)
    return jnp.clip(entries, min=-reach, max=reach).astype(kind)


def setup_inputs(seed: int = 0) -> dict:
    key_of = jax.random.split(jax.random.key(seed), 4)
    tokens = draw_tokens(jax.random.fold_in(key_of[3], 71), 0)
    w_qkv = scatter_about(key_of[1], (D, 3 * D), D ** -0.5, 0.375)
    w_out = scatter_about(key_of[2], (D, D), D ** -0.5, 0.375)
    return dict(tokens=tokens, w_qkv=w_qkv, w_out=w_out)


def attend_block(grid_block, w_qkv, w_out):
    lead_shape = grid_block.shape[:-1]
    model_width = grid_block.shape[-1]
    head_size = model_width // HEADS
    qkv = jnp.dot(grid_block.reshape(-1, model_width), w_qkv, preferred_element_type=jnp.float32).astype(jnp.bfloat16)
    qkv = qkv.reshape(lead_shape + (3, HEADS, head_size))
    query_part = qkv[..., 0, :, :].astype(jnp.float32)
    key_part = qkv[..., 1, :, :].astype(jnp.float32)
    value_part = qkv[..., 2, :, :].astype(jnp.float32)
    score_scale = 1.0 / math.sqrt(head_size)
    scores = jnp.einsum('guche,xyche->chguxy', query_part, key_part, precision=lax.Precision.HIGHEST) * score_scale
    row_max = lax.optimization_barrier(jnp.max(scores, axis=(-2, -1), keepdims=True))
    exponent = jnp.exp(scores - row_max)
    weights = (exponent / lax.optimization_barrier(jnp.sum(exponent, axis=(-2, -1), keepdims=True))).astype(jnp.bfloat16)
    mixed = jnp.einsum('chguxy,xyche->guche', weights.astype(jnp.float32), value_part, precision=lax.Precision.HIGHEST).astype(jnp.bfloat16)
    outputs = jnp.dot(mixed.reshape(-1, model_width), w_out, preferred_element_type=jnp.float32).astype(jnp.bfloat16)
    return outputs.reshape(lead_shape + (model_width,))

def reference(tokens, w_qkv, w_out):
    total_rows, total_cols, model_width = tokens.shape
    rows_grid = total_rows // GRID
    grid_view = tokens.reshape(GRID, rows_grid, total_cols, model_width)

    def one_row(index):
        picked = lax.dynamic_index_in_dim(grid_view, index, 1, keepdims=False)
        grid_block = picked.reshape(GRID, GRID, total_cols // GRID, model_width)
        return attend_block(grid_block, w_qkv, w_out)
    outputs = lax.map(one_row, jnp.arange(rows_grid, dtype=jnp.int32))
    return outputs.transpose(1, 0, 2, 3, 4).reshape(total_rows, total_cols, model_width)
```

```python
import functools
import math

import jax
import jax.numpy as jnp
import numpy as np
from jax import lax
from jax.experimental import pallas as pl
from jax.experimental.pallas import tpu as pltpu
from jax.sharding import PartitionSpec as P

HEADS = 8
GRID = 8
LANES = 128
F32 = jnp.float32
BF16 = jnp.bfloat16


def member_order(lat_count, lon_count):
    share = lat_count // GRID
    index = np.arange(lat_count * lon_count).reshape(4, 2, share, 2, lon_count // 2)
    index = index.transpose(2, 0, 1, 3, 4).reshape(share, 4, 4, lon_count // 2)
    lists = []
    for which in range(share):
        order = (2, 1, 0) if which % 2 == 0 else (0, 1, 2)
        lists.append(index[which].transpose(order).reshape(-1).tolist())
    return lists


def attend_half(query, key, value, masks, scale):
    members = query.shape[0]
    spread = jnp.concatenate([query * mask for mask in masks], axis=0)
    scores = lax.dot_general(key, spread, (((1,), (1,)), ((), ())), preferred_element_type=F32) * scale
    exponent = jnp.exp(scores - jnp.max(scores, axis=0, keepdims=True))
    total = jnp.sum(exponent, axis=0, keepdims=True)
    weights = (exponent * (1.0 / total)).astype(BF16)
    product = lax.dot_general(weights, value, (((0,), (0,)), ((), ())), preferred_element_type=F32)
    mixed = None
    for head, mask in enumerate(masks):
        term = product[head * members : (head + 1) * members] * mask.astype(F32)
        mixed = term if mixed is None else mixed + term
    return mixed.astype(BF16)


def attend_kernel(members, groups, unroll, tokens, w_qkv, w_out, out, *scratch):
    width = tokens.shape[-1]
    halves = width // LANES
    head_size = width // HEADS
    scale = 1.0 / math.sqrt(head_size)
    arrived, finished = scratch[:halves], scratch[halves:]
    for half in range(halves):
        part = tokens[:, :, half * LANES : (half + 1) * LANES]
        arrived[half][...] = part.reshape(members * groups, LANES).astype(F32)
    lane = lax.broadcasted_iota(jnp.int32, (1, LANES), 1)
    masks = [
        ((lane >= first) & (lane < first + head_size)).astype(F32).astype(BF16)
        for first in range(0, LANES, head_size)
    ]

    def step(index, carry):
        blocks = []
        for at in range(unroll):
            rows = pl.ds(index * unroll + at, members, stride=groups)
            blocks.append(jnp.concatenate([ref[rows, :].astype(BF16) for ref in arrived], axis=1))
        block = jnp.concatenate(blocks, axis=0)
        qkv = jnp.dot(block, w_qkv[...], preferred_element_type=F32).astype(BF16)
        mixed = []
        for at in range(unroll):
            rows = slice(at * members, (at + 1) * members)
            parts = []
            for half in range(halves):
                columns = [
                    slice(kind * width + half * LANES, kind * width + (half + 1) * LANES) for kind in range(3)
                ]
                parts.append(attend_half(*[qkv[rows, column] for column in columns], masks, scale))
            mixed.append(jnp.concatenate(parts, axis=1))
        result = jnp.dot(jnp.concatenate(mixed, axis=0), w_out[...], preferred_element_type=F32)
        for at in range(unroll):
            rows = pl.ds(index * unroll + at, members, stride=groups)
            for half in range(halves):
                finished[half][rows, :] = result[
                    at * members : (at + 1) * members, half * LANES : (half + 1) * LANES
                ]
        return carry

    lax.fori_loop(0, groups // unroll, step, 0)
    for half in range(halves):
        part = finished[half][...].astype(BF16).reshape(members, groups, LANES)
        out[:, :, half * LANES : (half + 1) * LANES] = part


def attend(tokens, w_qkv, w_out):
    members, groups, width = tokens.shape
    vmem = pl.BlockSpec(memory_space=pltpu.VMEM)
    return pl.pallas_call(
        functools.partial(attend_kernel, members, groups, 4),
        out_shape=jax.ShapeDtypeStruct(tokens.shape, BF16),
        in_specs=[vmem] * 3,
        out_specs=vmem,
        scratch_shapes=[pltpu.VMEM((members * groups, LANES), F32)] * (2 * width // LANES),
        compiler_params=pltpu.CompilerParams(vmem_limit_bytes=40 * 1024 * 1024),
    )(tokens, w_qkv, w_out)


def body(lists, tokens, w_qkv, w_out):
    rows, columns, width = tokens.shape
    members = len(lists[0])
    exchange = functools.partial(
        lax.all_to_all,
        axis_name=("lat", "lon"),
        split_axis=0,
        concat_axis=0,
        axis_index_groups=lists,
        tiled=True,
    )
    arrived = exchange(tokens.reshape(members, rows * columns // members, width))
    returned = exchange(attend(arrived, w_qkv, w_out))
    return returned.reshape(rows, columns, width)


def solution(mesh):
    lists = member_order(mesh.shape["lat"], mesh.shape["lon"])
    placed = (P("lat", "lon", None), P(), P())
    return jax.shard_map(
        functools.partial(body, lists),
        mesh=mesh,
        in_specs=placed,
        out_specs=P("lat", "lon", None),
        check_vma=False,
    )
```

```python
import functools
import math

import jax
import jax.numpy as jnp
import numpy as np
from jax import lax
from jax.experimental import pallas as pl
from jax.experimental.pallas import tpu as pltpu
from jax.sharding import PartitionSpec as P

HEADS = 8
GRID = 8
LANES = 128
F32 = jnp.float32
BF16 = jnp.bfloat16


def member_order(lat_count, lon_count):
    share = lat_count // GRID
    index = np.arange(lat_count * lon_count).reshape(4, 2, share, 2, lon_count // 2)
    index = index.transpose(2, 0, 1, 3, 4).reshape(share, 4, 4, lon_count // 2)
    lists = []
    for which in range(share):
        order = (2, 1, 0) if which % 2 == 0 else (0, 1, 2)
        lists.append(index[which].transpose(order).reshape(-1).tolist())
    return lists


def attend_scores(query, key, masks):
    spread = jnp.concatenate([key * mask for mask in masks], axis=0)
    return lax.dot_general(query, spread, (((1,), (1,)), ((), ())), preferred_element_type=F32)


def exponentials(scores, factor):
    first = lax.broadcasted_iota(jnp.int32, (scores.shape[0], LANES), 1) < LANES // 2
    tiles = []
    for at in range(0, scores.shape[1], LANES):
        tile = scores[:, at : at + LANES]
        low = jnp.max(jnp.where(first, tile, -jnp.inf), axis=1, keepdims=True)
        high = jnp.max(jnp.where(first, -jnp.inf, tile), axis=1, keepdims=True)
        tiles.append(jnp.exp2((tile - jnp.where(first, low, high)) * factor).astype(BF16))
    return jnp.concatenate(tiles, axis=1)


def mix_values(exponent, value, masks, ones):
    spread = jnp.concatenate([value * mask for mask in masks], axis=0)
    both = jnp.dot(exponent, jnp.concatenate([spread, ones], axis=1), preferred_element_type=F32)
    return (both[:, :LANES] * (1.0 / both[:, LANES:])).astype(BF16)


def attend_kernel(members, groups, unroll, pitch, tokens, w_qkv, w_out, out, *scratch):
    width = tokens.shape[-1]
    halves = width // LANES
    head_size = width // HEADS
    factor = math.log2(math.e) / math.sqrt(head_size)
    arrived, finished = scratch[:halves], scratch[halves:]
    for half in range(halves):
        for member in range(members):
            part = tokens[member, :, half * LANES : (half + 1) * LANES]
            arrived[half][member * pitch : member * pitch + groups, :] = part.astype(F32)
    lane = lax.broadcasted_iota(jnp.int32, (1, LANES), 1)
    masks = [
        ((lane >= first) & (lane < first + head_size)).astype(F32).astype(BF16)
        for first in range(0, LANES, head_size)
    ]
    ones = jnp.concatenate([jnp.broadcast_to(mask, (members, LANES)) for mask in masks], axis=0)

    def step(index, carry):
        blocks = []
        for at in range(unroll):
            rows = pl.ds(index * unroll + at, members, stride=pitch)
            blocks.append(jnp.concatenate([ref[rows, :].astype(BF16) for ref in arrived], axis=1))
        block = jnp.concatenate(blocks, axis=0)
        qkv = jnp.dot(block, w_qkv[...], preferred_element_type=F32).astype(BF16)
        cells = [(at, half) for at in range(unroll) for half in range(halves)]

        def piece(cell, kind):
            at, half = cell
            left = kind * width + half * LANES
            return qkv[at * members : (at + 1) * members, left : left + LANES]

        scores = [attend_scores(piece(cell, 0), piece(cell, 1), masks) for cell in cells]
        exponents = [exponentials(score, factor) for score in scores]
        mixed = [mix_values(exponents[n], piece(cell, 2), masks, ones) for n, cell in enumerate(cells)]
        joined = [jnp.concatenate(mixed[n : n + halves], axis=1) for n in range(0, len(mixed), halves)]
        result = jnp.dot(jnp.concatenate(joined, axis=0), w_out[...], preferred_element_type=F32)
        for at in range(unroll):
            rows = pl.ds(index * unroll + at, members, stride=pitch)
            for half in range(halves):
                finished[half][rows, :] = result[
                    at * members : (at + 1) * members, half * LANES : (half + 1) * LANES
                ]
        return carry

    lax.fori_loop(0, groups // unroll, step, 0)
    for half in range(halves):
        for member in range(members):
            part = finished[half][member * pitch : member * pitch + groups, :].astype(BF16)
            out[member, :, half * LANES : (half + 1) * LANES] = part


def attend(tokens, w_qkv, w_out):
    members, groups, width = tokens.shape
    pitch = groups + 8
    vmem = pl.BlockSpec(memory_space=pltpu.VMEM)
    return pl.pallas_call(
        functools.partial(attend_kernel, members, groups, 16, pitch),
        out_shape=jax.ShapeDtypeStruct(tokens.shape, BF16),
        in_specs=[vmem] * 3,
        out_specs=vmem,
        scratch_shapes=[pltpu.VMEM((members * pitch, LANES), F32)] * (2 * width // LANES),
        compiler_params=pltpu.CompilerParams(vmem_limit_bytes=40 * 1024 * 1024),
    )(tokens, w_qkv, w_out)


def body(lists, tokens, w_qkv, w_out):
    rows, columns, width = tokens.shape
    members = len(lists[0])
    exchange = functools.partial(
        lax.all_to_all,
        axis_name=("lat", "lon"),
        split_axis=0,
        concat_axis=0,
        axis_index_groups=lists,
        tiled=True,
    )
    arrived = exchange(tokens.reshape(members, rows * columns // members, width))
    returned = exchange(attend(arrived, w_qkv, w_out))
    return returned.reshape(rows, columns, width)


def solution(mesh):
    lists = member_order(mesh.shape["lat"], mesh.shape["lon"])
    placed = (P("lat", "lon", None), P(), P())
    return jax.shard_map(
        functools.partial(body, lists),
        mesh=mesh,
        in_specs=placed,
        out_specs=P("lat", "lon", None),
        check_vma=False,
    )
```

```python
import functools
import math

import jax
import jax.numpy as jnp
import numpy as np
from jax import lax
from jax.experimental import pallas as pl
from jax.experimental.pallas import tpu as pltpu
from jax.sharding import PartitionSpec as P

HEADS = 8
GRID = 8
LANES = 128
F32 = jnp.float32
BF16 = jnp.bfloat16


def member_order(lat_count, lon_count):
    share = lat_count // GRID
    index = np.arange(lat_count * lon_count).reshape(4, 2, share, 2, lon_count // 2)
    index = index.transpose(2, 0, 1, 3, 4).reshape(share, 4, 4, lon_count // 2)
    return index.transpose(0, 3, 1, 2).reshape(share, -1).tolist()


def attend_scores(query, key, masks):
    spread = jnp.concatenate([key * mask for mask in masks], axis=0)
    return lax.dot_general(query, spread, (((1,), (1,)), ((), ())), preferred_element_type=F32)


def exponentials(scores, factor):
    first = lax.broadcasted_iota(jnp.int32, (scores.shape[0], LANES), 1) < LANES // 2
    tiles = []
    for at in range(0, scores.shape[1], LANES):
        tile = scores[:, at : at + LANES]
        low = jnp.max(jnp.where(first, tile, -jnp.inf), axis=1, keepdims=True)
        high = jnp.max(jnp.where(first, -jnp.inf, tile), axis=1, keepdims=True)
        tiles.append(jnp.exp2((tile - jnp.where(first, low, high)) * factor).astype(BF16))
    return jnp.concatenate(tiles, axis=1)


def mix_values(exponent, value, masks, ones):
    spread = jnp.concatenate([value * mask for mask in masks], axis=0)
    both = jnp.dot(exponent, jnp.concatenate([spread, ones], axis=1), preferred_element_type=F32)
    return (both[:, :LANES] * (1.0 / both[:, LANES:])).astype(BF16)


def attend_kernel(members, groups, unroll, pitch, tokens, w_qkv, w_out, out, *scratch):
    width = tokens.shape[-1]
    halves = width // LANES
    head_size = width // HEADS
    factor = math.log2(math.e) / math.sqrt(head_size)
    arrived, finished = scratch[:halves], scratch[halves:]
    for half in range(halves):
        for member in range(members):
            part = tokens[member, :, half * LANES : (half + 1) * LANES]
            arrived[half][member * pitch : member * pitch + groups, :] = part.astype(F32)
    lane = lax.broadcasted_iota(jnp.int32, (1, LANES), 1)
    masks = [
        ((lane >= first) & (lane < first + head_size)).astype(F32).astype(BF16)
        for first in range(0, LANES, head_size)
    ]
    ones = jnp.concatenate([jnp.broadcast_to(mask, (members, LANES)) for mask in masks], axis=0)

    def step(index, carry):
        blocks = []
        for at in range(unroll):
            rows = pl.ds(index * unroll + at, members, stride=pitch)
            blocks.append(jnp.concatenate([ref[rows, :].astype(BF16) for ref in arrived], axis=1))
        block = jnp.concatenate(blocks, axis=0)
        qkv = jnp.dot(block, w_qkv[...], preferred_element_type=F32).astype(BF16)
        cells = [(at, half) for at in range(unroll) for half in range(halves)]

        def piece(cell, kind):
            at, half = cell
            left = kind * width + half * LANES
            return qkv[at * members : (at + 1) * members, left : left + LANES]

        scores = [attend_scores(piece(cell, 0), piece(cell, 1), masks) for cell in cells]
        exponents = [exponentials(score, factor) for score in scores]
        mixed = [mix_values(exponents[n], piece(cell, 2), masks, ones) for n, cell in enumerate(cells)]
        joined = [jnp.concatenate(mixed[n : n + halves], axis=1) for n in range(0, len(mixed), halves)]
        result = jnp.dot(jnp.concatenate(joined, axis=0), w_out[...], preferred_element_type=F32)
        for at in range(unroll):
            rows = pl.ds(index * unroll + at, members, stride=pitch)
            for half in range(halves):
                finished[half][rows, :] = result[
                    at * members : (at + 1) * members, half * LANES : (half + 1) * LANES
                ]
        return carry

    lax.fori_loop(0, groups // unroll, step, 0)
    for half in range(halves):
        for member in range(members):
            part = finished[half][member * pitch : member * pitch + groups, :].astype(BF16)
            out[member, :, half * LANES : (half + 1) * LANES] = part


def attend(tokens, w_qkv, w_out):
    members, groups, width = tokens.shape
    pitch = groups + 8
    vmem = pl.BlockSpec(memory_space=pltpu.VMEM)
    return pl.pallas_call(
        functools.partial(attend_kernel, members, groups, groups, pitch),
        out_shape=jax.ShapeDtypeStruct(tokens.shape, BF16),
        in_specs=[vmem] * 3,
        out_specs=vmem,
        scratch_shapes=[pltpu.VMEM((members * pitch, LANES), F32)] * (2 * width // LANES),
        compiler_params=pltpu.CompilerParams(vmem_limit_bytes=40 * 1024 * 1024),
    )(tokens, w_qkv, w_out)


def body(lists, tokens, w_qkv, w_out):
    rows, columns, width = tokens.shape
    members = len(lists[0])
    exchange = functools.partial(
        lax.all_to_all,
        axis_name=("lat", "lon"),
        split_axis=0,
        concat_axis=0,
        axis_index_groups=lists,
        tiled=True,
    )
    arrived = exchange(tokens.reshape(members, rows * columns // members, width))
    returned = exchange(attend(arrived, w_qkv, w_out))
    return returned.reshape(rows, columns, width)


def solution(mesh):
    lists = member_order(mesh.shape["lat"], mesh.shape["lon"])
    placed = (P("lat", "lon", None), P(), P())
    return jax.shard_map(
        functools.partial(body, lists),
        mesh=mesh,
        in_specs=placed,
        out_specs=P("lat", "lon", None),
        check_vma=False,
    )
```

```python
import functools
import math

import jax
import jax.numpy as jnp
import numpy as np
from jax import lax
from jax.experimental import pallas as pl
from jax.experimental.pallas import tpu as pltpu
from jax.sharding import PartitionSpec as P

HEADS = 8
GRID = 8
LANES = 128
F32 = jnp.float32
BF16 = jnp.bfloat16


def member_order(lat_count, lon_count):
    share = lat_count // GRID
    index = np.arange(lat_count * lon_count).reshape(4, 2, share, 2, lon_count // 2)
    index = index.transpose(2, 0, 1, 3, 4).reshape(share, 4, 4, lon_count // 2)
    lists = []
    for which in range(share):
        chips = np.roll(index[which], 2 * which, (0, 1, 2))
        lists.append(chips.transpose(2, 0, 1).reshape(-1).tolist())
    return lists


def attend_scores(query, key, masks):
    spread = jnp.concatenate([key * mask for mask in masks], axis=0)
    return lax.dot_general(query, spread, (((1,), (1,)), ((), ())), preferred_element_type=F32)


def exponentials(scores, factor):
    first = lax.broadcasted_iota(jnp.int32, (scores.shape[0], LANES), 1) < LANES // 2
    tiles = []
    for at in range(0, scores.shape[1], LANES):
        tile = scores[:, at : at + LANES]
        low = jnp.max(jnp.where(first, tile, -jnp.inf), axis=1, keepdims=True)
        high = jnp.max(jnp.where(first, -jnp.inf, tile), axis=1, keepdims=True)
        tiles.append(jnp.exp2((tile - jnp.where(first, low, high)) * factor).astype(BF16))
    return jnp.concatenate(tiles, axis=1)


def mix_values(exponent, value, masks, ones):
    spread = jnp.concatenate([value * mask for mask in masks], axis=0)
    both = jnp.dot(exponent, jnp.concatenate([spread, ones], axis=1), preferred_element_type=F32)
    return (both[:, :LANES] * (1.0 / both[:, LANES:])).astype(BF16)


def attend_kernel(members, groups, unroll, pitch, tokens, w_qkv, w_out, out, *scratch):
    width = tokens.shape[-1]
    halves = width // LANES
    head_size = width // HEADS
    factor = math.log2(math.e) / math.sqrt(head_size)
    arrived, finished = scratch[:halves], scratch[halves:]
    for half in range(halves):
        for member in range(members):
            part = tokens[member, :, half * LANES : (half + 1) * LANES]
            arrived[half][member * pitch : member * pitch + groups, :] = part.astype(F32)
    lane = lax.broadcasted_iota(jnp.int32, (1, LANES), 1)
    masks = [
        ((lane >= first) & (lane < first + head_size)).astype(F32).astype(BF16)
        for first in range(0, LANES, head_size)
    ]
    ones = jnp.concatenate([jnp.broadcast_to(mask, (members, LANES)) for mask in masks], axis=0)

    def step(index, carry):
        blocks = []
        for at in range(unroll):
            rows = pl.ds(index * unroll + at, members, stride=pitch)
            blocks.append(jnp.concatenate([ref[rows, :].astype(BF16) for ref in arrived], axis=1))
        block = jnp.concatenate(blocks, axis=0)
        qkv = jnp.dot(block, w_qkv[...], preferred_element_type=F32).astype(BF16)
        cells = [(at, half) for at in range(unroll) for half in range(halves)]

        def piece(cell, kind):
            at, half = cell
            left = kind * width + half * LANES
            return qkv[at * members : (at + 1) * members, left : left + LANES]

        scores = [attend_scores(piece(cell, 0), piece(cell, 1), masks) for cell in cells]
        exponents = [exponentials(score, factor) for score in scores]
        mixed = [mix_values(exponents[n], piece(cell, 2), masks, ones) for n, cell in enumerate(cells)]
        joined = [jnp.concatenate(mixed[n : n + halves], axis=1) for n in range(0, len(mixed), halves)]
        result = jnp.dot(jnp.concatenate(joined, axis=0), w_out[...], preferred_element_type=F32)
        for at in range(unroll):
            rows = pl.ds(index * unroll + at, members, stride=pitch)
            for half in range(halves):
                finished[half][rows, :] = result[
                    at * members : (at + 1) * members, half * LANES : (half + 1) * LANES
                ]
        return carry

    lax.fori_loop(0, groups // unroll, step, 0)
    for half in range(halves):
        for member in range(members):
            part = finished[half][member * pitch : member * pitch + groups, :].astype(BF16)
            out[member, :, half * LANES : (half + 1) * LANES] = part


def attend(tokens, w_qkv, w_out):
    members, groups, width = tokens.shape
    pitch = groups + 8
    vmem = pl.BlockSpec(memory_space=pltpu.VMEM)
    return pl.pallas_call(
        functools.partial(attend_kernel, members, groups, groups, pitch),
        out_shape=jax.ShapeDtypeStruct(tokens.shape, BF16),
        in_specs=[vmem] * 3,
        out_specs=vmem,
        scratch_shapes=[pltpu.VMEM((members * pitch, LANES), F32)] * (2 * width // LANES),
        compiler_params=pltpu.CompilerParams(vmem_limit_bytes=40 * 1024 * 1024),
    )(tokens, w_qkv, w_out)


def body(lists, tokens, w_qkv, w_out):
    rows, columns, width = tokens.shape
    members = len(lists[0])
    exchange = functools.partial(
        lax.all_to_all,
        axis_name=("lat", "lon"),
        split_axis=0,
        concat_axis=0,
        axis_index_groups=lists,
        tiled=True,
    )
    arrived = exchange(tokens.reshape(members, rows * columns // members, width))
    returned = exchange(attend(arrived, w_qkv, w_out))
    return returned.reshape(rows, columns, width)


def solution(mesh):
    lists = member_order(mesh.shape["lat"], mesh.shape["lon"])
    placed = (P("lat", "lon", None), P(), P())
    return jax.shard_map(
        functools.partial(body, lists),
        mesh=mesh,
        in_specs=placed,
        out_specs=P("lat", "lon", None),
        check_vma=False,
    )
```

```python
import functools
import math

import jax
import jax.numpy as jnp
import numpy as np
from jax import lax
from jax.experimental import pallas as pl
from jax.experimental.pallas import tpu as pltpu
from jax.sharding import PartitionSpec as P

HEADS = 8
GRID = 8
LANES = 128
F32 = jnp.float32
BF16 = jnp.bfloat16


def member_order(lat_count, lon_count):
    share = lat_count // GRID
    index = np.arange(lat_count * lon_count).reshape(4, 2, share, 2, lon_count // 2)
    index = index.transpose(2, 0, 1, 3, 4).reshape(share, 4, 4, lon_count // 2)
    lists = []
    for which in range(share):
        chips = np.roll(index[which], 2 * which, (0, 1, 2))
        lists.append(chips.transpose(0, 2, 1).reshape(-1).tolist())
    return lists


def attend_scores(query, key, masks):
    spread = jnp.concatenate([key * mask for mask in masks], axis=0)
    return lax.dot_general(query, spread, (((1,), (1,)), ((), ())), preferred_element_type=F32)


def exponentials(scores, factor):
    first = lax.broadcasted_iota(jnp.int32, (scores.shape[0], LANES), 1) < LANES // 2
    tiles = []
    for at in range(0, scores.shape[1], LANES):
        tile = scores[:, at : at + LANES]
        low = jnp.max(jnp.where(first, tile, -jnp.inf), axis=1, keepdims=True)
        high = jnp.max(jnp.where(first, -jnp.inf, tile), axis=1, keepdims=True)
        tiles.append(jnp.exp2((tile - jnp.where(first, low, high)) * factor).astype(BF16))
    return jnp.concatenate(tiles, axis=1)


def mix_values(exponent, value, masks, ones):
    spread = jnp.concatenate([value * mask for mask in masks], axis=0)
    both = jnp.dot(exponent, jnp.concatenate([spread, ones], axis=1), preferred_element_type=F32)
    return (both[:, :LANES] * (1.0 / both[:, LANES:])).astype(BF16)


def attend_kernel(members, groups, unroll, pitch, tokens, w_qkv, w_out, out, *scratch):
    width = tokens.shape[-1]
    halves = width // LANES
    head_size = width // HEADS
    factor = math.log2(math.e) / math.sqrt(head_size)
    arrived, finished = scratch[:halves], scratch[halves:]
    for half in range(halves):
        for member in range(members):
            part = tokens[member, :, half * LANES : (half + 1) * LANES]
            arrived[half][member * pitch : member * pitch + groups, :] = part.astype(F32)
    lane = lax.broadcasted_iota(jnp.int32, (1, LANES), 1)
    masks = [
        ((lane >= first) & (lane < first + head_size)).astype(F32).astype(BF16)
        for first in range(0, LANES, head_size)
    ]
    ones = jnp.concatenate([jnp.broadcast_to(mask, (members, LANES)) for mask in masks], axis=0)

    def step(index, carry):
        blocks = []
        for at in range(unroll):
            rows = pl.ds(index * unroll + at, members, stride=pitch)
            blocks.append(jnp.concatenate([ref[rows, :].astype(BF16) for ref in arrived], axis=1))
        block = jnp.concatenate(blocks, axis=0)
        qkv = jnp.dot(block, w_qkv[...], preferred_element_type=F32).astype(BF16)
        cells = [(at, half) for at in range(unroll) for half in range(halves)]

        def piece(cell, kind):
            at, half = cell
            left = kind * width + half * LANES
            return qkv[at * members : (at + 1) * members, left : left + LANES]

        scores = [attend_scores(piece(cell, 0), piece(cell, 1), masks) for cell in cells]
        exponents = [exponentials(score, factor) for score in scores]
        mixed = [mix_values(exponents[n], piece(cell, 2), masks, ones) for n, cell in enumerate(cells)]
        joined = [jnp.concatenate(mixed[n : n + halves], axis=1) for n in range(0, len(mixed), halves)]
        result = jnp.dot(jnp.concatenate(joined, axis=0), w_out[...], preferred_element_type=F32)
        for at in range(unroll):
            rows = pl.ds(index * unroll + at, members, stride=pitch)
            for half in range(halves):
                finished[half][rows, :] = result[
                    at * members : (at + 1) * members, half * LANES : (half + 1) * LANES
                ]
        return carry

    lax.fori_loop(0, groups // unroll, step, 0)
    for half in range(halves):
        for member in range(members):
            part = finished[half][member * pitch : member * pitch + groups, :].astype(BF16)
            out[member, :, half * LANES : (half + 1) * LANES] = part


def attend(tokens, w_qkv, w_out):
    members, groups, width = tokens.shape
    pitch = groups + 8
    vmem = pl.BlockSpec(memory_space=pltpu.VMEM)
    return pl.pallas_call(
        functools.partial(attend_kernel, members, groups, groups, pitch),
        out_shape=jax.ShapeDtypeStruct(tokens.shape, BF16),
        in_specs=[vmem] * 3,
        out_specs=vmem,
        scratch_shapes=[pltpu.VMEM((members * pitch, LANES), F32)] * (2 * width // LANES),
        compiler_params=pltpu.CompilerParams(vmem_limit_bytes=40 * 1024 * 1024),
    )(tokens, w_qkv, w_out)


def body(lists, tokens, w_qkv, w_out):
    rows, columns, width = tokens.shape
    members = len(lists[0])
    exchange = functools.partial(
        lax.all_to_all,
        axis_name=("lat", "lon"),
        split_axis=0,
        concat_axis=0,
        axis_index_groups=lists,
        tiled=True,
    )
    arrived = exchange(tokens.reshape(members, rows * columns // members, width))
    returned = exchange(attend(arrived, w_qkv, w_out))
    return returned.reshape(rows, columns, width)


def solution(mesh):
    lists = member_order(mesh.shape["lat"], mesh.shape["lon"])
    placed = (P("lat", "lon", None), P(), P())
    return jax.shard_map(
        functools.partial(body, lists),
        mesh=mesh,
        in_specs=placed,
        out_specs=P("lat", "lon", None),
        check_vma=False,
    )
```

```python
import functools
import math

import jax
import jax.numpy as jnp
import numpy as np
from jax import lax
from jax.experimental import pallas as pl
from jax.experimental.pallas import tpu as pltpu
from jax.sharding import PartitionSpec as P

HEADS = 8
GRID = 8
LANES = 128
F32 = jnp.float32
BF16 = jnp.bfloat16


def member_order(lat_count, lon_count):
    share = lat_count // GRID
    index = np.arange(lat_count * lon_count).reshape(4, 2, share, 2, lon_count // 2)
    index = index.transpose(2, 0, 1, 3, 4).reshape(share, 4, 4, lon_count // 2)
    lists = []
    for which in range(share):
        chips = np.roll(index[which], 2 * which, (0, 1, 2))
        lists.append(chips.transpose(1, 0, 2).reshape(-1).tolist())
    return lists


def attend_scores(query, key, masks):
    spread = jnp.concatenate([key * mask for mask in masks], axis=0)
    return lax.dot_general(query, spread, (((1,), (1,)), ((), ())), preferred_element_type=F32)


def exponentials(scores, factor):
    first = lax.broadcasted_iota(jnp.int32, (scores.shape[0], LANES), 1) < LANES // 2
    tiles = []
    for at in range(0, scores.shape[1], LANES):
        tile = scores[:, at : at + LANES]
        low = jnp.max(jnp.where(first, tile, -jnp.inf), axis=1, keepdims=True)
        high = jnp.max(jnp.where(first, -jnp.inf, tile), axis=1, keepdims=True)
        tiles.append(jnp.exp2((tile - jnp.where(first, low, high)) * factor).astype(BF16))
    return jnp.concatenate(tiles, axis=1)


def mix_values(exponent, value, masks, ones):
    spread = jnp.concatenate([value * mask for mask in masks], axis=0)
    both = jnp.dot(exponent, jnp.concatenate([spread, ones], axis=1), preferred_element_type=F32)
    return (both[:, :LANES] * (1.0 / both[:, LANES:])).astype(BF16)


def attend_kernel(members, groups, unroll, pitch, tokens, w_qkv, w_out, out, *scratch):
    width = tokens.shape[-1]
    halves = width // LANES
    head_size = width // HEADS
    factor = math.log2(math.e) / math.sqrt(head_size)
    arrived, finished = scratch[:halves], scratch[halves:]
    for half in range(halves):
        for member in range(members):
            part = tokens[member, :, half * LANES : (half + 1) * LANES]
            arrived[half][member * pitch : member * pitch + groups, :] = part.astype(F32)
    lane = lax.broadcasted_iota(jnp.int32, (1, LANES), 1)
    masks = [
        ((lane >= first) & (lane < first + head_size)).astype(F32).astype(BF16)
        for first in range(0, LANES, head_size)
    ]
    ones = jnp.concatenate([jnp.broadcast_to(mask, (members, LANES)) for mask in masks], axis=0)

    def step(index, carry):
        blocks = []
        for at in range(unroll):
            rows = pl.ds(index * unroll + at, members, stride=pitch)
            blocks.append(jnp.concatenate([ref[rows, :].astype(BF16) for ref in arrived], axis=1))
        block = jnp.concatenate(blocks, axis=0)
        qkv = jnp.dot(block, w_qkv[...], preferred_element_type=F32).astype(BF16)
        cells = [(at, half) for at in range(unroll) for half in range(halves)]

        def piece(cell, kind):
            at, half = cell
            left = kind * width + half * LANES
            return qkv[at * members : (at + 1) * members, left : left + LANES]

        scores = [attend_scores(piece(cell, 0), piece(cell, 1), masks) for cell in cells]
        exponents = [exponentials(score, factor) for score in scores]
        mixed = [mix_values(exponents[n], piece(cell, 2), masks, ones) for n, cell in enumerate(cells)]
        joined = [jnp.concatenate(mixed[n : n + halves], axis=1) for n in range(0, len(mixed), halves)]
        result = jnp.dot(jnp.concatenate(joined, axis=0), w_out[...], preferred_element_type=F32)
        for at in range(unroll):
            rows = pl.ds(index * unroll + at, members, stride=pitch)
            for half in range(halves):
                finished[half][rows, :] = result[
                    at * members : (at + 1) * members, half * LANES : (half + 1) * LANES
                ]
        return carry

    lax.fori_loop(0, groups // unroll, step, 0)
    for half in range(halves):
        for member in range(members):
            part = finished[half][member * pitch : member * pitch + groups, :].astype(BF16)
            out[member, :, half * LANES : (half + 1) * LANES] = part


def attend(tokens, w_qkv, w_out):
    members, groups, width = tokens.shape
    pitch = groups + 8
    vmem = pl.BlockSpec(memory_space=pltpu.VMEM)
    return pl.pallas_call(
        functools.partial(attend_kernel, members, groups, groups, pitch),
        out_shape=jax.ShapeDtypeStruct(tokens.shape, BF16),
        in_specs=[vmem] * 3,
        out_specs=vmem,
        scratch_shapes=[pltpu.VMEM((members * pitch, LANES), F32)] * (2 * width // LANES),
        compiler_params=pltpu.CompilerParams(vmem_limit_bytes=40 * 1024 * 1024),
    )(tokens, w_qkv, w_out)


def body(lists, tokens, w_qkv, w_out):
    rows, columns, width = tokens.shape
    members = len(lists[0])
    exchange = functools.partial(
        lax.all_to_all,
        axis_name=("lat", "lon"),
        split_axis=0,
        concat_axis=0,
        axis_index_groups=lists,
        tiled=True,
    )
    arrived = exchange(tokens.reshape(members, rows * columns // members, width))
    returned = exchange(attend(arrived, w_qkv, w_out))
    return returned.reshape(rows, columns, width)


def solution(mesh):
    lists = member_order(mesh.shape["lat"], mesh.shape["lon"])
    placed = (P("lat", "lon", None), P(), P())
    return jax.shard_map(
        functools.partial(body, lists),
        mesh=mesh,
        in_specs=placed,
        out_specs=P("lat", "lon", None),
        check_vma=False,
    )
```

```python
import functools
import math

import jax
import jax.numpy as jnp
import numpy as np
from jax import lax
from jax.experimental import pallas as pl
from jax.experimental.pallas import tpu as pltpu
from jax.sharding import PartitionSpec as P

HEADS = 8
GRID = 8
LANES = 128
F32 = jnp.float32
BF16 = jnp.bfloat16


def member_order(lat_count, lon_count):
    share = lat_count // GRID
    index = np.arange(lat_count * lon_count).reshape(4, 2, share, 2, lon_count // 2)
    index = index.transpose(2, 0, 1, 3, 4).reshape(share, 4, 4, lon_count // 2)
    lists = []
    for which in range(share):
        chips = np.roll(index[which], which, (0, 1, 2))
        lists.append(chips.transpose(1, 0, 2).reshape(-1).tolist())
    return lists


def attend_scores(query, key, masks):
    spread = jnp.concatenate([key * mask for mask in masks], axis=0)
    return lax.dot_general(query, spread, (((1,), (1,)), ((), ())), preferred_element_type=F32)


def exponentials(scores, factor):
    first = lax.broadcasted_iota(jnp.int32, (scores.shape[0], LANES), 1) < LANES // 2
    tiles = []
    for at in range(0, scores.shape[1], LANES):
        tile = scores[:, at : at + LANES]
        low = jnp.max(jnp.where(first, tile, -jnp.inf), axis=1, keepdims=True)
        high = jnp.max(jnp.where(first, -jnp.inf, tile), axis=1, keepdims=True)
        tiles.append(jnp.exp2((tile - jnp.where(first, low, high)) * factor).astype(BF16))
    return jnp.concatenate(tiles, axis=1)


def mix_values(exponent, value, masks, ones):
    spread = jnp.concatenate([value * mask for mask in masks], axis=0)
    both = jnp.dot(exponent, jnp.concatenate([spread, ones], axis=1), preferred_element_type=F32)
    return (both[:, :LANES] * (1.0 / both[:, LANES:])).astype(BF16)


def attend_kernel(members, groups, unroll, pitch, tokens, w_qkv, w_out, out, *scratch):
    width = tokens.shape[-1]
    halves = width // LANES
    head_size = width // HEADS
    factor = math.log2(math.e) / math.sqrt(head_size)
    arrived, finished = scratch[:halves], scratch[halves:]
    for half in range(halves):
        for member in range(members):
            part = tokens[member, :, half * LANES : (half + 1) * LANES]
            arrived[half][member * pitch : member * pitch + groups, :] = part.astype(F32)
    lane = lax.broadcasted_iota(jnp.int32, (1, LANES), 1)
    masks = [
        ((lane >= first) & (lane < first + head_size)).astype(F32).astype(BF16)
        for first in range(0, LANES, head_size)
    ]
    ones = jnp.concatenate([jnp.broadcast_to(mask, (members, LANES)) for mask in masks], axis=0)

    def step(index, carry):
        blocks = []
        for at in range(unroll):
            rows = pl.ds(index * unroll + at, members, stride=pitch)
            blocks.append(jnp.concatenate([ref[rows, :].astype(BF16) for ref in arrived], axis=1))
        block = jnp.concatenate(blocks, axis=0)
        qkv = jnp.dot(block, w_qkv[...], preferred_element_type=F32).astype(BF16)
        cells = [(at, half) for at in range(unroll) for half in range(halves)]

        def piece(cell, kind):
            at, half = cell
            left = kind * width + half * LANES
            return qkv[at * members : (at + 1) * members, left : left + LANES]

        scores = [attend_scores(piece(cell, 0), piece(cell, 1), masks) for cell in cells]
        exponents = [exponentials(score, factor) for score in scores]
        mixed = [mix_values(exponents[n], piece(cell, 2), masks, ones) for n, cell in enumerate(cells)]
        joined = [jnp.concatenate(mixed[n : n + halves], axis=1) for n in range(0, len(mixed), halves)]
        result = jnp.dot(jnp.concatenate(joined, axis=0), w_out[...], preferred_element_type=F32)
        for at in range(unroll):
            rows = pl.ds(index * unroll + at, members, stride=pitch)
            for half in range(halves):
                finished[half][rows, :] = result[
                    at * members : (at + 1) * members, half * LANES : (half + 1) * LANES
                ]
        return carry

    lax.fori_loop(0, groups // unroll, step, 0)
    for half in range(halves):
        for member in range(members):
            part = finished[half][member * pitch : member * pitch + groups, :].astype(BF16)
            out[member, :, half * LANES : (half + 1) * LANES] = part


def attend(tokens, w_qkv, w_out):
    members, groups, width = tokens.shape
    pitch = groups + 8
    vmem = pl.BlockSpec(memory_space=pltpu.VMEM)
    return pl.pallas_call(
        functools.partial(attend_kernel, members, groups, groups, pitch),
        out_shape=jax.ShapeDtypeStruct(tokens.shape, BF16),
        in_specs=[vmem] * 3,
        out_specs=vmem,
        scratch_shapes=[pltpu.VMEM((members * pitch, LANES), F32)] * (2 * width // LANES),
        compiler_params=pltpu.CompilerParams(vmem_limit_bytes=40 * 1024 * 1024),
    )(tokens, w_qkv, w_out)


def body(lists, tokens, w_qkv, w_out):
    rows, columns, width = tokens.shape
    members = len(lists[0])
    exchange = functools.partial(
        lax.all_to_all,
        axis_name=("lat", "lon"),
        split_axis=0,
        concat_axis=0,
        axis_index_groups=lists,
        tiled=True,
    )
    arrived = exchange(tokens.reshape(members, rows * columns // members, width))
    returned = exchange(attend(arrived, w_qkv, w_out))
    return returned.reshape(rows, columns, width)


def solution(mesh):
    lists = member_order(mesh.shape["lat"], mesh.shape["lon"])
    placed = (P("lat", "lon", None), P(), P())
    return jax.shard_map(
        functools.partial(body, lists),
        mesh=mesh,
        in_specs=placed,
        out_specs=P("lat", "lon", None),
        check_vma=False,
    )
```
